256 devices in a mesh: var: 64 (over x_lo, z, y), samp: 4 (over x_hi, core).
Axes of the slice: x: 4 (x_hi: 2, x_lo: 2; x = x_hi * 2 + x_lo), y: 4, z: 8, core: 2. Of those that a mesh axis runs over, the one named last changes fastest.
Arguments:
- dosages: bfloat16 [8192, 49152], P('samp', 'var'), may hold values from 0 to 2
- observed: int32 [8192, 49152], P('samp', 'var'), may hold values 0 or 1
Outputs:
- ld_scores: float32 [49152], P(('var', 'samp'))
The draws below stay inside these ranges and needn't reach their ends.
All inputs are finite; a program needn't handle non-finite values. No bound on the sum of `observed` on one device may be relied on, other than what follows from the above.
Results may differ from the reference program's by a relative error of at most 0.00055.
Values may be sent and summed in bfloat16 or wider, within the bound.
A program may use at most 192 MiB of HBM per device.

```python
import jax
import jax.numpy as jnp
from jax import lax

BLK = 768
BAND = 3
SAMPLES = 8192
VARIANTS = 49152


def draw_dosages(key, part):
    subkeys = jax.random.split(key, 12)
    positions = jnp.arange(VARIANTS)
    latent = jax.random.normal(subkeys[0], (SAMPLES, VARIANTS), jnp.float32)
    for level, seg_len in enumerate((BLK // 2, 2 * BLK, 4 * BLK)):
        offset = jax.random.randint(subkeys[1 + level], (), 0, seg_len)
        seg_count = VARIANTS // seg_len + 2
        factor = jax.random.normal(subkeys[4 + level], (SAMPLES, seg_count), jnp.float32)
        loading = jnp.exp(jax.random.uniform(subkeys[7 + level], (VARIANTS,), jnp.float32, -1.0, 0.5))
        latent = latent + factor[:, (positions + offset) // seg_len] * loading
    center = jax.random.uniform(subkeys[11], (VARIANTS,), jnp.float32, -1.5, 1.5)
    return (2.0 * jax.nn.sigmoid(0.6 * latent + center)).astype(jnp.bfloat16)


def touch_ends(entries, key, low, high):
    longest = entries.shape.index(max(entries.shape))
    spots = []
    for shift in (0, 1):
        where = [jax.random.randint(jax.random.fold_in(key, axis), (), 0, length) for axis, length in enumerate(entries.shape)]
        where[longest] = (where[longest] + shift) % entries.shape[longest]
        spots.append(tuple(where))
    return entries.at[spots[0]].set(low).at[spots[1]].set(high)


def setup_inputs(seed: int = 0) -> dict:
    seeds = jax.random.split(jax.random.key(seed), 3)
    return {
        "dosages": draw_dosages(jax.random.fold_in(seeds[2], 71), 0),
        "observed": touch_ends((jax.random.randint(seeds[1], (SAMPLES, VARIANTS), 0, 10) < 9).astype(jnp.int32), jax.random.fold_in(seeds[1], 1), 0, 1),
    }


def standardize(dose_block, mask_block):
    values = dose_block.astype(jnp.float32)
    present = mask_block.astype(jnp.float32)
    seen_count = jnp.maximum(lax.optimization_barrier(jnp.sum(present, 0)), 1.0)
    column_mean = lax.optimization_barrier(jnp.sum(present * values, 0)) / seen_count
    spread = lax.optimization_barrier(jnp.sum(present * values * values, 0)) / seen_count - column_mean * column_mean
    return ((values - column_mean) * lax.rsqrt(spread + 1e-05) * present).astype(jnp.bfloat16)

def adjusted_r2(gram_part):
    correl = gram_part / SAMPLES
    squared = correl * correl
    return squared - (1.0 - squared) / (SAMPLES - 2)

def reference(dosages, observed):
    block_count = VARIANTS // BLK
    dosage_blocks = dosages.reshape(SAMPLES, block_count, BLK).transpose(1, 0, 2)
    mask_blocks = observed.reshape(SAMPLES, block_count, BLK).transpose(1, 0, 2)
    standard = lax.map(lambda pair_in: standardize(pair_in[0], pair_in[1]), (dosage_blocks, mask_blocks))
    padded = jnp.concatenate([standard, jnp.zeros((BAND, SAMPLES, BLK), jnp.bfloat16)], 0)

    def one_block(block_id):
        own_block = lax.dynamic_index_in_dim(standard, block_id, 0, keepdims=False)
        row_sums = jnp.zeros((BLK,), jnp.float32)
        col_list = []
        for offset in range(BAND + 1):
            partner = lax.dynamic_index_in_dim(padded, block_id + offset, 0, keepdims=False)
            gram_part = lax.dot_general(own_block, partner, (((0,), (0,)), ((), ())), preferred_element_type=jnp.float32)
            in_range = (block_id + offset < block_count).astype(jnp.float32)
            adjusted = adjusted_r2(gram_part) * in_range
            row_sums = row_sums + lax.optimization_barrier(jnp.sum(adjusted, 1))
            if offset > 0:
                col_list.append(lax.optimization_barrier(jnp.sum(adjusted, 0)))
        return (row_sums, jnp.stack(col_list))
    row_sums, col_sums = lax.map(one_block, jnp.arange(block_count, dtype=jnp.int32))
    col_padded = jnp.concatenate([jnp.zeros((BAND, BAND, BLK), jnp.float32), col_sums], 0)
    ld_total = row_sums
    for offset in range(1, BAND + 1):
        ld_total = ld_total + col_padded[BAND - offset:BAND - offset + block_count, offset - 1]
    return (ld_total / BLK).reshape(VARIANTS)
```

```python
import functools

import jax
import jax.numpy as jnp
from jax import lax
from jax.experimental import pallas as pl
from jax.experimental.pallas import tpu as pltpu
from jax.sharding import PartitionSpec as P

MESH = pl.DeviceIdType.MESH
BAND = 3
LANES = 128
RING = 4
PIECES = 2
F32 = jnp.float32
BF16 = jnp.bfloat16


def plan(chunks):
    width = chunks * LANES
    units = [("own", k, width, 2 * LANES) for k in range(chunks // 2)]
    for j in range(chunks):
        units.append(("both", j, width, 2 * LANES))
        units.append(("down", j, LANES * (j + 1), LANES))
        if j:
            units.append(("across", j, LANES, LANES * j))
    return units


def kernel(chain, units, dose_hbm, seen_hbm, out_ref, dose, seen, own, near, far, relay, stat, stat_in,
           row_own, row_near, col_near, col_far, share, share_in, *rest):
    count = len(units)
    part, half_out, half_in, quarter_out, quarter_in = [rest[i * count:(i + 1) * count] for i in range(5)]
    (load_sem, stat_send, stat_recv, near_send, near_recv, far_send, far_recv, hop_send, hop_recv, relay_send,
     half_send, half_recv, quarter_send, quarter_recv, share_send, share_recv) = rest[5 * count:]
    depth, width = dose.shape
    chunks = width // LANES
    quarter = width // 4
    samples = 4 * depth
    v = lax.axis_index("var")
    s = lax.axis_index("samp")
    core = lax.rem(s, 2)
    side = s // 2
    y = lax.rem(v, RING)
    first_in_ring = y == 0
    last_in_ring = y == RING - 1

    def at(step, member=None):
        return (lax.rem(v + step + chain, chain), s if member is None else member)

    mate = (v, s + 1 - 2 * core)
    opposite = (v, lax.rem(s + 2, 4))

    def cols(j):
        return pl.ds(j * LANES, LANES)

    loads = []
    for j in range(chunks):
        loads.append((
            pltpu.make_async_copy(dose_hbm.at[:, cols(j)], dose.at[:, cols(j)], load_sem.at[0, j]),
            pltpu.make_async_copy(seen_hbm.at[:, cols(j)], seen.at[:, cols(j)], load_sem.at[1, j])))
        for copy in loads[-1]:
            copy.start()

    barrier = pltpu.get_barrier_semaphore()
    friends = [(v, lax.rem(s + k, 4)) for k in (1, 2, 3)]
    for step in (1, 3):
        friends += [at(step, q) for q in range(4)] + [at(-step, q) for q in range(4)]
    friends += [at(4), at(-4)]
    for friend in friends:
        pl.semaphore_signal(barrier, inc=1, device_id=friend, device_id_type=MESH)

    row_own[...] = jnp.zeros_like(row_own)
    row_near[...] = jnp.zeros_like(row_near)
    col_near[...] = jnp.zeros_like(col_near)
    col_far[...] = jnp.zeros_like(col_far)

    block = min(256, depth)

    def sum_chunk(j):
        def body(r, acc):
            rows = pl.ds(pl.multiple_of(r * block, block), block)
            present = seen[rows, cols(j)].astype(F32)
            values = dose[rows, cols(j)].astype(F32)
            weighted = present * values
            terms = (present, weighted, weighted * values)
            return tuple(a + jnp.sum(t.reshape(block // 8, 8, LANES), 0) for a, t in zip(acc, terms))

        zero = jnp.zeros((8, LANES), F32)
        sums = lax.fori_loop(0, depth // block, body, (zero, zero, zero))
        for i, total in enumerate(sums):
            stat[j, i:i + 1, :] = jnp.sum(total, 0, keepdims=True)

    def stat_copy(j, k):
        return pltpu.make_async_remote_copy(
            src_ref=stat.at[j], dst_ref=stat_in.at[k - 1, j], send_sem=stat_send.at[k - 1, j],
            recv_sem=stat_recv.at[k - 1, j], device_id=(v, lax.rem(s + k, 4)), device_id_type=MESH)

    def piece(ref, j, p):
        rows = depth // PIECES
        return ref.at[pl.ds(p * rows, rows), cols(j)]

    def near_copy(j):
        return pltpu.make_async_remote_copy(
            src_ref=own.at[:, cols(j)], dst_ref=near.at[:, cols(j)], send_sem=near_send.at[j],
            recv_sem=near_recv.at[j], device_id=at(-1), device_id_type=MESH)

    def hop_copy(j, p):
        return pltpu.make_async_remote_copy(
            src_ref=piece(own, j, p), dst_ref=piece(relay, j, p), send_sem=hop_send.at[j, p],
            recv_sem=hop_recv.at[j, p], device_id=at(3), device_id_type=MESH)

    def relay_copy(j, p):
        return pltpu.make_async_remote_copy(
            src_ref=piece(relay, j, p), dst_ref=piece(near, j, p), send_sem=relay_send.at[j, p],
            recv_sem=near_recv.at[j], device_id=at(-4), device_id_type=MESH)

    def far_copy(j):
        return pltpu.make_async_remote_copy(
            src_ref=own.at[:, cols(j)], dst_ref=far.at[:, cols(j)], send_sem=far_send.at[j],
            recv_sem=far_recv.at[j], device_id=at(-3), device_id_type=MESH)

    def standardize(j):
        for k in (1, 2, 3):
            stat_copy(j, k).wait_recv()
        sums = stat[j] + stat_in[0, j] + stat_in[1, j] + stat_in[2, j]
        seen_count = jnp.maximum(sums[0:1], 1.0)
        mean = sums[1:2] / seen_count
        spread = sums[2:3] / seen_count - mean * mean
        scale = lax.rsqrt(spread + 1e-05)

        def body(r, carry):
            rows = pl.ds(pl.multiple_of(r * block, block), block)
            present = seen[rows, cols(j)].astype(F32)
            values = dose[rows, cols(j)].astype(F32)
            own[rows, cols(j)] = ((values - mean) * scale * present).astype(BF16)
            return carry

        lax.fori_loop(0, depth // block, body, 0)
        far_copy(j).start()

        @pl.when(first_in_ring)
        def _():
            for p in range(PIECES):
                hop_copy(j, p).start()

        @pl.when(jnp.logical_not(first_in_ring))
        def _():
            near_copy(j).start()

    for j in range(chunks + 2):
        if j < chunks:
            for copy in loads[j]:
                copy.wait()
            stat[j] = jnp.zeros((8, LANES), F32)
            sum_chunk(j)
            if j == 0:
                pl.semaphore_wait(barrier, len(friends))
            for k in (1, 2, 3):
                stat_copy(j, k).start()
        if j >= 2:
            standardize(j - 2)

    keep_near = jnp.where(v + 1 < chain, 1.0, 0.0).astype(F32)
    keep_far = jnp.where(v + 3 < chain, 1.0, 0.0).astype(F32)
    keep_cross = jnp.where(lax.rem(v + 1, chain) + 2 < chain, 1.0, 0.0).astype(F32)

    def dot(a, b):
        return lax.dot_general(a, b, (((0,), (0,)), ((), ())), preferred_element_type=F32)

    def half_copy(u):
        return pltpu.make_async_remote_copy(
            src_ref=half_out[u], dst_ref=half_in[u], send_sem=half_send.at[u], recv_sem=half_recv.at[u],
            device_id=mate, device_id_type=MESH)

    def quarter_copy(u):
        return pltpu.make_async_remote_copy(
            src_ref=quarter_out[u], dst_ref=quarter_in[u], send_sem=quarter_send.at[u],
            recv_sem=quarter_recv.at[u], device_id=opposite, device_id_type=MESH)

    def rows_of(u, index):
        size = units[u][2] // 4
        return pl.ds(pl.multiple_of(index * size, size), size)

    def multiply(u):
        kind, j, _, _ = units[u]
        if kind == "own":
            part[u][...] = dot(own[...], own[:, 2 * j * LANES:2 * (j + 1) * LANES])
        elif kind == "both":
            part[u][...] = dot(own[...], jnp.concatenate([near[:, cols(j)], far[:, cols(j)]], 1))
        elif kind == "down":
            part[u][...] = dot(near[:, :LANES * (j + 1)], far[:, cols(j)])
        else:
            part[u][...] = dot(near[:, cols(j)], far[:, :LANES * j])
        for p in range(2):
            half_out[u][p] = part[u][rows_of(u, 2 * p + 1 - core), :].astype(BF16)
        half_copy(u).start()

    def fold_mate(u):
        half_copy(u).wait_recv()
        away = rows_of(u, 2 * (1 - side) + core)
        quarter_out[u][...] = (part[u][away, :] + half_in[u][1 - side].astype(F32)).astype(BF16)
        quarter_copy(u).start()
        home = rows_of(u, s)
        part[u][home, :] = part[u][home, :] + half_in[u][side].astype(F32)

    def by_lane(x):
        total = x[:, :LANES]
        for i in range(1, x.shape[1] // LANES):
            total = total + x[:, i * LANES:(i + 1) * LANES]
        return total

    def by_sublane(x):
        return jnp.sum(x.reshape(x.shape[0] // 8, 8, x.shape[1]), 0)

    def fold_opposite(u):
        quarter_copy(u).wait_recv()
        kind, j, rows, columns = units[u]
        total = part[u][rows_of(u, s), :] + quarter_in[u][...].astype(F32)
        square = total * total
        if kind == "own":
            row_own[:quarter, :] += by_lane(square)
        elif kind == "both":
            to_near = square[:, :LANES] * keep_near
            to_far = square[:, LANES:] * keep_far
            row_own[:quarter, :] += to_near + to_far
            col_near[:, cols(j)] += by_sublane(to_near)
            col_far[:, cols(j)] += by_sublane(to_far)
        else:
            square = square * keep_cross
            size = rows // 4
            start = s * size if kind == "down" else LANES * j + s * size
            where = pl.ds(pl.multiple_of(start, size), size)
            row_near[where, :] += by_lane(square)
            if kind == "down":
                col_far[:, cols(j)] += by_sublane(square)
            else:
                col_far[:, :columns] += by_sublane(square)

    def arrive(j):
        @pl.when(last_in_ring)
        def _():
            for p in range(PIECES):
                hop_copy(j, p).wait_recv()
                relay_copy(j, p).start()

        far_copy(j).wait_recv()
        near_copy(j).wait_recv()

    for u in range(count + 2):
        if u < count:
            if units[u][0] == "both":
                arrive(units[u][1])
            multiply(u)
        if 1 <= u <= count:
            fold_mate(u - 1)
        if u >= 2:
            fold_opposite(u - 2)

    near_sum = jnp.sum(row_near[...].T, 0, keepdims=True) + jnp.sum(col_near[...], 0, keepdims=True)
    far_sum = jnp.sum(col_far[...], 0, keepdims=True)

    def share_copy(i, q):
        return pltpu.make_async_remote_copy(
            src_ref=share.at[i, q], dst_ref=share_in.at[i, s], send_sem=share_send.at[i, q],
            recv_sem=share_recv.at[i, s], device_id=at((1, 3)[i], q), device_id_type=MESH)

    def share_arrival(i, q):
        return pltpu.make_async_remote_copy(
            src_ref=share.at[i, q], dst_ref=share_in.at[i, q], send_sem=share_send.at[i, q],
            recv_sem=share_recv.at[i, q], device_id=at((1, 3)[i], q), device_id_type=MESH)

    for i, total in enumerate((near_sum, far_sum)):
        wide = jnp.broadcast_to(total, (8, width))
        for q in range(4):
            turned = wide if q == 0 else pltpu.roll(wide, width - q * quarter, 1)
            share[i, q] = turned[:, :2 * LANES]
            share_copy(i, q).start()
    row_total = jnp.sum(row_own[...].T, 0, keepdims=True)
    for i in range(2):
        for q in range(4):
            share_arrival(i, q).wait_recv()
            row_total = row_total + share_in[i, q, 0:1, :]
    pairs = (1 + jnp.minimum(v, BAND) + jnp.minimum(chain - 1 - v, BAND)).astype(F32)
    squares = row_total * (1.0 / (samples * samples))
    result = squares / width + (squares / width - pairs) / (samples - 2)
    out_ref[...] = result[:, :quarter]

    for j in range(chunks):
        for k in (1, 2, 3):
            stat_copy(j, k).wait_send()
        far_copy(j).wait_send()

    @pl.when(first_in_ring)
    def _():
        for j in range(chunks):
            for p in range(PIECES):
                hop_copy(j, p).wait_send()

    @pl.when(jnp.logical_not(first_in_ring))
    def _():
        for j in range(chunks):
            near_copy(j).wait_send()

    @pl.when(last_in_ring)
    def _():
        for j in range(chunks):
            for p in range(PIECES):
                relay_copy(j, p).wait_send()

    for u in range(count):
        half_copy(u).wait_send()
        quarter_copy(u).wait_send()
    for i in range(2):
        for q in range(4):
            share_copy(i, q).wait_send()


def local(chain, dosages, observed):
    depth, width = dosages.shape
    chunks = width // LANES
    units = plan(chunks)
    count = len(units)
    dma = pltpu.SemaphoreType.DMA
    scratch = [
        pltpu.VMEM((depth, width), BF16),
        pltpu.VMEM((depth, width), jnp.int32),
        pltpu.VMEM((depth, width), BF16),
        pltpu.VMEM((depth, width), BF16),
        pltpu.VMEM((depth, width), BF16),
        pltpu.VMEM((depth, width), BF16),
        pltpu.VMEM((chunks, 8, LANES), F32),
        pltpu.VMEM((3, chunks, 8, LANES), F32),
        pltpu.VMEM((2 * LANES, LANES), F32),
        pltpu.VMEM((width, LANES), F32),
        pltpu.VMEM((8, width), F32),
        pltpu.VMEM((8, width), F32),
        pltpu.VMEM((2, 4, 8, 2 * LANES), F32),
        pltpu.VMEM((2, 4, 8, 2 * LANES), F32),
    ]
    scratch += [pltpu.VMEM((rows, columns), F32) for _, _, rows, columns in units]
    for _ in range(2):
        scratch += [pltpu.VMEM((2, rows // 4, columns), BF16) for _, _, rows, columns in units]
    for _ in range(2):
        scratch += [pltpu.VMEM((rows // 4, columns), BF16) for _, _, rows, columns in units]
    scratch += [
        dma((2, chunks)), dma((3, chunks)), dma((3, chunks)),
        dma((chunks,)), dma((chunks,)), dma((chunks,)), dma((chunks,)),
        dma((chunks, PIECES)), dma((chunks, PIECES)), dma((chunks, PIECES)),
        dma((count,)), dma((count,)), dma((count,)), dma((count,)),
        dma((2, 4)), dma((2, 4)),
    ]
    out = pl.pallas_call(
        functools.partial(kernel, chain, units),
        out_shape=jax.ShapeDtypeStruct((1, width // 4), F32),
        in_specs=[pl.BlockSpec(memory_space=pl.ANY)] * 2,
        out_specs=pl.BlockSpec(memory_space=pltpu.VMEM),
        scratch_shapes=scratch,
        compiler_params=pltpu.CompilerParams(
            collective_id=0, has_side_effects=True, vmem_limit_bytes=56 * 2**20),
    )(dosages, observed)
    return out.reshape(width // 4)


def solution(mesh):
    placed = (P("samp", "var"), P("samp", "var"))
    return jax.shard_map(
        functools.partial(local, mesh.shape["var"]), mesh=mesh, in_specs=placed,
        out_specs=P(("var", "samp")), check_vma=False)
```

```python
import functools

import jax
import jax.numpy as jnp
from jax import lax
from jax.experimental import pallas as pl
from jax.experimental.pallas import tpu as pltpu
from jax.sharding import PartitionSpec as P

MESH = pl.DeviceIdType.MESH
BAND = 3
LANES = 128
RING = 4
PIECES = 4
F32 = jnp.float32
BF16 = jnp.bfloat16


def plan(chunks):
    width = chunks * LANES
    units = [("own", k, width, 2 * LANES) for k in range(chunks // 2)]
    for j in range(chunks):
        units.append(("both", j, width, 2 * LANES))
        units.append(("down", j, LANES * (j + 1), LANES))
        if j:
            units.append(("across", j, LANES, LANES * j))
    return units


def kernel(chain, units, dose_hbm, seen_hbm, out_ref, dose, seen, own, near, far, relay, stat, stat_in,
           row_own, row_near, col_near, col_far, share, share_in, *rest):
    count = len(units)
    part, half_out, half_in, quarter_out, quarter_in = [rest[i * count:(i + 1) * count] for i in range(5)]
    (load_sem, stat_send, stat_recv, near_send, near_recv, far_send, far_recv, edge_send, hop_send, hop_recv, relay_send,
     half_send, half_recv, quarter_send, quarter_recv, share_send, share_recv) = rest[5 * count:]
    depth, width = dose.shape
    chunks = width // LANES
    quarter = width // 4
    samples = 4 * depth
    v = lax.axis_index("var")
    s = lax.axis_index("samp")
    core = lax.rem(s, 2)
    side = s // 2
    y = lax.rem(v, RING)
    edge = lax.rem(v, chain // 2) < RING
    leaves = jnp.logical_and(edge, y != RING - 1)
    lands = jnp.logical_and(lax.rem(v, chain // 2) >= chain // 2 - RING, y != RING - 1)
    first_in_ring = y == 0
    last_in_ring = y == RING - 1

    def at(step, member=None):
        return (lax.rem(v + step + chain, chain), s if member is None else member)

    mate = (v, s + 1 - 2 * core)
    opposite = (v, lax.rem(s + 2, 4))

    def cols(j):
        return pl.ds(j * LANES, LANES)

    loads = []
    for j in range(chunks):
        loads.append((
            pltpu.make_async_copy(dose_hbm.at[:, cols(j)], dose.at[:, cols(j)], load_sem.at[0, j]),
            pltpu.make_async_copy(seen_hbm.at[:, cols(j)], seen.at[:, cols(j)], load_sem.at[1, j])))
        for copy in loads[-1]:
            copy.start()

    barrier = pltpu.get_barrier_semaphore()
    friends = [(v, lax.rem(s + k, 4)) for k in (1, 2, 3)]
    for step in (1, 3):
        friends += [at(step, q) for q in range(4)] + [at(-step, q) for q in range(4)]
    friends += [at(4), at(-4)]
    across = chain // 2
    if across > 4:
        friends += [at(step) for step in (across + 3, -across - 3, across - 4, 4 - across, across + 1, -across - 1)]
    for friend in friends:
        pl.semaphore_signal(barrier, inc=1, device_id=friend, device_id_type=MESH)

    row_own[...] = jnp.zeros_like(row_own)
    row_near[...] = jnp.zeros_like(row_near)
    col_near[...] = jnp.zeros_like(col_near)
    col_far[...] = jnp.zeros_like(col_far)

    block = min(256, depth)

    def sum_chunk(j):
        def body(r, acc):
            rows = pl.ds(pl.multiple_of(r * block, block), block)
            present = seen[rows, cols(j)].astype(F32)
            values = dose[rows, cols(j)].astype(F32)
            weighted = present * values
            terms = (present, weighted, weighted * values)
            return tuple(a + jnp.sum(t.reshape(block // 8, 8, LANES), 0) for a, t in zip(acc, terms))

        zero = jnp.zeros((8, LANES), F32)
        sums = lax.fori_loop(0, depth // block, body, (zero, zero, zero))
        for i, total in enumerate(sums):
            stat[j, i:i + 1, :] = jnp.sum(total, 0, keepdims=True)

    def stat_copy(j, k):
        return pltpu.make_async_remote_copy(
            src_ref=stat.at[j], dst_ref=stat_in.at[k - 1, j], send_sem=stat_send.at[k - 1, j],
            recv_sem=stat_recv.at[k - 1, j], device_id=(v, lax.rem(s + k, 4)), device_id_type=MESH)

    def piece(ref, j, p):
        rows = depth // PIECES
        return ref.at[pl.ds(p * rows, rows), cols(j)]

    def near_copy(j):
        return pltpu.make_async_remote_copy(
            src_ref=own.at[:, cols(j)], dst_ref=near.at[:, cols(j)], send_sem=near_send.at[j],
            recv_sem=near_recv.at[j], device_id=at(-1), device_id_type=MESH)

    def hop_copy(j, p):
        return pltpu.make_async_remote_copy(
            src_ref=piece(own, j, p), dst_ref=piece(relay, j, p), send_sem=hop_send.at[j, p],
            recv_sem=hop_recv.at[j, p], device_id=at(jnp.where(edge, across + 3, 3) if p < 1 else 3), device_id_type=MESH)

    def relay_copy(j, p, target, sem, step):
        return pltpu.make_async_remote_copy(
            src_ref=piece(relay, j, p), dst_ref=piece(target, j, p), send_sem=relay_send.at[j, p],
            recv_sem=sem.at[j], device_id=at(step), device_id_type=MESH)

    def near_relay(j, p):
        return relay_copy(j, p, near, near_recv, jnp.where(edge, across - 4, -4) if p < 1 else -4)

    def far_relay(j, p):
        return relay_copy(j, p, far, far_recv, across + 1)

    def far_copy(j):
        return pltpu.make_async_remote_copy(
            src_ref=own.at[:, cols(j)], dst_ref=far.at[:, cols(j)], send_sem=far_send.at[j],
            recv_sem=far_recv.at[j], device_id=at(-3), device_id_type=MESH)

    def direct_copy(j, p):
        return pltpu.make_async_remote_copy(
            src_ref=piece(own, j, p), dst_ref=piece(far, j, p), send_sem=edge_send.at[j, p],
            recv_sem=far_recv.at[j], device_id=at(-3), device_id_type=MESH)

    def cross_copy(j, p):
        return pltpu.make_async_remote_copy(
            src_ref=piece(own, j, p), dst_ref=piece(relay, j, p), send_sem=edge_send.at[j, p],
            recv_sem=hop_recv.at[j, p], device_id=at(across - 4), device_id_type=MESH)

    def each_send(j, act):
        @pl.when(jnp.logical_not(leaves))
        def _():
            act(far_copy(j))

        @pl.when(leaves)
        def _():
            for p in range(2):
                act(cross_copy(j, p))
                act(direct_copy(j, p + 2))

        @pl.when(first_in_ring)
        def _():
            for p in range(PIECES):
                act(hop_copy(j, p))

        @pl.when(jnp.logical_not(first_in_ring))
        def _():
            act(near_copy(j))

    def standardize(j):
        for k in (1, 2, 3):
            stat_copy(j, k).wait_recv()
        sums = stat[j] + stat_in[0, j] + stat_in[1, j] + stat_in[2, j]
        seen_count = jnp.maximum(sums[0:1], 1.0)
        mean = sums[1:2] / seen_count
        spread = sums[2:3] / seen_count - mean * mean
        scale = lax.rsqrt(spread + 1e-05)

        def body(r, carry):
            rows = pl.ds(pl.multiple_of(r * block, block), block)
            present = seen[rows, cols(j)].astype(F32)
            values = dose[rows, cols(j)].astype(F32)
            own[rows, cols(j)] = ((values - mean) * scale * present).astype(BF16)
            return carry

        lax.fori_loop(0, depth // block, body, 0)

        each_send(j, lambda copy: copy.start())

    hops = [(j, p) for j in range(chunks) for p in range(PIECES)]
    passed = []

    def pass_on(until):
        ready = [hop for hop in hops if hop < until and hop not in passed]
        passed.extend(ready)

        @pl.when(last_in_ring)
        def _():
            for j, p in ready:
                hop_copy(j, p).wait_recv()
                near_relay(j, p).start()

        @pl.when(lands)
        def _():
            for j, p in ready:
                if p < 2:
                    hop_copy(j, p).wait_recv()
                    far_relay(j, p).start()

    for j in range(chunks + 2):
        if j < chunks:
            for copy in loads[j]:
                copy.wait()
            stat[j] = jnp.zeros((8, LANES), F32)
            sum_chunk(j)
            if j == 0:
                pl.semaphore_wait(barrier, len(friends))
            for k in (1, 2, 3):
                stat_copy(j, k).start()
        if j >= 2:
            standardize(j - 2)
        if j >= chunks:
            pass_on((0, j - chunks + 1))

    keep_near = jnp.where(v + 1 < chain, 1.0, 0.0).astype(F32)
    keep_far = jnp.where(v + 3 < chain, 1.0, 0.0).astype(F32)
    keep_cross = jnp.where(lax.rem(v + 1, chain) + 2 < chain, 1.0, 0.0).astype(F32)

    def dot(a, b):
        return lax.dot_general(a, b, (((0,), (0,)), ((), ())), preferred_element_type=F32)

    def half_copy(u):
        return pltpu.make_async_remote_copy(
            src_ref=half_out[u], dst_ref=half_in[u], send_sem=half_send.at[u], recv_sem=half_recv.at[u],
            device_id=mate, device_id_type=MESH)

    def quarter_copy(u):
        return pltpu.make_async_remote_copy(
            src_ref=quarter_out[u], dst_ref=quarter_in[u], send_sem=quarter_send.at[u],
            recv_sem=quarter_recv.at[u], device_id=opposite, device_id_type=MESH)

    def rows_of(u, index):
        size = units[u][2] // 4
        return pl.ds(pl.multiple_of(index * size, size), size)

    def multiply(u):
        kind, j, _, _ = units[u]
        if kind == "own":
            part[u][...] = dot(own[...], own[:, 2 * j * LANES:2 * (j + 1) * LANES])
        elif kind == "both":
            part[u][...] = dot(own[...], jnp.concatenate([near[:, cols(j)], far[:, cols(j)]], 1))
        elif kind == "down":
            part[u][...] = dot(near[:, :LANES * (j + 1)], far[:, cols(j)])
        else:
            part[u][...] = dot(near[:, cols(j)], far[:, :LANES * j])
        for p in range(2):
            half_out[u][p] = part[u][rows_of(u, 2 * p + 1 - core), :].astype(BF16)
        half_copy(u).start()

    def fold_mate(u):
        half_copy(u).wait_recv()
        away = rows_of(u, 2 * (1 - side) + core)
        quarter_out[u][...] = (part[u][away, :] + half_in[u][1 - side].astype(F32)).astype(BF16)
        quarter_copy(u).start()
        home = rows_of(u, s)
        part[u][home, :] = part[u][home, :] + half_in[u][side].astype(F32)

    def by_lane(x):
        total = x[:, :LANES]
        for i in range(1, x.shape[1] // LANES):
            total = total + x[:, i * LANES:(i + 1) * LANES]
        return total

    def by_sublane(x):
        return jnp.sum(x.reshape(x.shape[0] // 8, 8, x.shape[1]), 0)

    def fold_opposite(u):
        quarter_copy(u).wait_recv()
        kind, j, rows, columns = units[u]
        total = part[u][rows_of(u, s), :] + quarter_in[u][...].astype(F32)
        square = total * total
        if kind == "own":
            row_own[:quarter, :] += by_lane(square)
        elif kind == "both":
            to_near = square[:, :LANES] * keep_near
            to_far = square[:, LANES:] * keep_far
            row_own[:quarter, :] += to_near + to_far
            col_near[:, cols(j)] += by_sublane(to_near)
            col_far[:, cols(j)] += by_sublane(to_far)
        else:
            square = square * keep_cross
            size = rows // 4
            start = s * size if kind == "down" else LANES * j + s * size
            where = pl.ds(pl.multiple_of(start, size), size)
            row_near[where, :] += by_lane(square)
            if kind == "down":
                col_far[:, cols(j)] += by_sublane(square)
            else:
                col_far[:, :columns] += by_sublane(square)

    groups = [[u for u in range(count) if units[u][0] == "own"]]
    for j in range(chunks):
        groups.append([u for u in range(count) if units[u][0] != "own" and units[u][1] == j])
    to_mate, to_opposite = [], []

    def drain(group):
        while to_opposite and to_opposite[0][0] <= group:
            fold_opposite(to_opposite.pop(0)[1])

    for g, group in enumerate(groups):
        if g:
            pass_on((g, PIECES - 1))
            far_copy(g - 1).wait_recv()
            near_copy(g - 1).wait_recv()
        for i, u in enumerate(group):
            multiply(u)
            if to_mate:
                done = to_mate.pop(0)
                fold_mate(done[1])
                to_opposite.append(done)
            to_mate.append((g, u))
            pass_on((g, i + 2))
            drain(g - 4)
        pass_on((g, PIECES))
    for done in to_mate:
        fold_mate(done[1])
        to_opposite.append(done)
    drain(chunks)

    near_sum = jnp.sum(row_near[...].T, 0, keepdims=True) + jnp.sum(col_near[...], 0, keepdims=True)
    far_sum = jnp.sum(col_far[...], 0, keepdims=True)

    def share_copy(i, q):
        return pltpu.make_async_remote_copy(
            src_ref=share.at[i, q], dst_ref=share_in.at[i, s], send_sem=share_send.at[i, q],
            recv_sem=share_recv.at[i, s], device_id=at((1, 3)[i], q), device_id_type=MESH)

    def share_arrival(i, q):
        return pltpu.make_async_remote_copy(
            src_ref=share.at[i, q], dst_ref=share_in.at[i, q], send_sem=share_send.at[i, q],
            recv_sem=share_recv.at[i, q], device_id=at((1, 3)[i], q), device_id_type=MESH)

    for i, total in enumerate((near_sum, far_sum)):
        wide = jnp.broadcast_to(total, (8, width))
        for q in range(4):
            turned = wide if q == 0 else pltpu.roll(wide, width - q * quarter, 1)
            share[i, q] = turned[:, :2 * LANES]
            share_copy(i, q).start()
    row_total = jnp.sum(row_own[...].T, 0, keepdims=True)
    for i in range(2):
        for q in range(4):
            share_arrival(i, q).wait_recv()
            row_total = row_total + share_in[i, q, 0:1, :]
    pairs = (1 + jnp.minimum(v, BAND) + jnp.minimum(chain - 1 - v, BAND)).astype(F32)
    squares = row_total * (1.0 / (samples * samples))
    result = squares / width + (squares / width - pairs) / (samples - 2)
    out_ref[...] = result[:, :quarter]

    for j in range(chunks):
        for k in (1, 2, 3):
            stat_copy(j, k).wait_send()
        each_send(j, lambda copy: copy.wait_send())

    @pl.when(last_in_ring)
    def _():
        for j, p in hops:
            near_relay(j, p).wait_send()

    @pl.when(lands)
    def _():
        for j, p in hops:
            if p < 2:
                far_relay(j, p).wait_send()

    for u in range(count):
        half_copy(u).wait_send()
        quarter_copy(u).wait_send()
    for i in range(2):
        for q in range(4):
            share_copy(i, q).wait_send()


def local(chain, dosages, observed):
    depth, width = dosages.shape
    chunks = width // LANES
    units = plan(chunks)
    count = len(units)
    dma = pltpu.SemaphoreType.DMA
    scratch = [
        pltpu.VMEM((depth, width), BF16),
        pltpu.VMEM((depth, width), jnp.int32),
        pltpu.VMEM((depth, width), BF16),
        pltpu.VMEM((depth, width), BF16),
        pltpu.VMEM((depth, width), BF16),
        pltpu.VMEM((depth, width), BF16),
        pltpu.VMEM((chunks, 8, LANES), F32),
        pltpu.VMEM((3, chunks, 8, LANES), F32),
        pltpu.VMEM((2 * LANES, LANES), F32),
        pltpu.VMEM((width, LANES), F32),
        pltpu.VMEM((8, width), F32),
        pltpu.VMEM((8, width), F32),
        pltpu.VMEM((2, 4, 8, 2 * LANES), F32),
        pltpu.VMEM((2, 4, 8, 2 * LANES), F32),
    ]
    scratch += [pltpu.VMEM((rows, columns), F32) for _, _, rows, columns in units]
    for _ in range(2):
        scratch += [pltpu.VMEM((2, rows // 4, columns), BF16) for _, _, rows, columns in units]
    for _ in range(2):
        scratch += [pltpu.VMEM((rows // 4, columns), BF16) for _, _, rows, columns in units]
    scratch += [
        dma((2, chunks)), dma((3, chunks)), dma((3, chunks)),
        dma((chunks,)), dma((chunks,)), dma((chunks,)), dma((chunks,)),
        dma((chunks, PIECES)), dma((chunks, PIECES)), dma((chunks, PIECES)), dma((chunks, PIECES)),
        dma((count,)), dma((count,)), dma((count,)), dma((count,)),
        dma((2, 4)), dma((2, 4)),
    ]
    out = pl.pallas_call(
        functools.partial(kernel, chain, units),
        out_shape=jax.ShapeDtypeStruct((1, width // 4), F32),
        in_specs=[pl.BlockSpec(memory_space=pl.ANY)] * 2,
        out_specs=pl.BlockSpec(memory_space=pltpu.VMEM),
        scratch_shapes=scratch,
        compiler_params=pltpu.CompilerParams(
            collective_id=0, has_side_effects=True, vmem_limit_bytes=56 * 2**20),
    )(dosages, observed)
    return out.reshape(width // 4)


def solution(mesh):
    placed = (P("samp", "var"), P("samp", "var"))
    return jax.shard_map(
        functools.partial(local, mesh.shape["var"]), mesh=mesh, in_specs=placed,
        out_specs=P(("var", "samp")), check_vma=False)
```

```python
import functools

import jax
import jax.numpy as jnp
from jax import lax
from jax.experimental import pallas as pl
from jax.experimental.pallas import tpu as pltpu
from jax.sharding import PartitionSpec as P

MESH = pl.DeviceIdType.MESH
BAND = 3
LANES = 128
RING = 4
PIECES = 4
NEAR_SIDE = 1
FAR_SIDE = (1, 2)
F32 = jnp.float32
BF16 = jnp.bfloat16


def plan(chunks):
    width = chunks * LANES
    units = [("own", k, width, 2 * LANES) for k in range(chunks // 2)]
    for j in range(chunks):
        units.append(("both", j, width, 2 * LANES))
        units.append(("down", j, LANES * (j + 1), LANES))
        if j:
            units.append(("across", j, LANES, LANES * j))
    return units


def kernel(chain, units, dose_hbm, seen_hbm, out_ref, dose, seen, own, near, far, relay, stat, stat_in,
           row_own, row_near, col_near, col_far, share, share_in, *rest):
    count = len(units)
    part, half_out, half_in, quarter_out, quarter_in = [rest[i * count:(i + 1) * count] for i in range(5)]
    (load_sem, stat_send, stat_recv, near_send, near_recv, far_send, far_recv, edge_send, hop_send, hop_recv, relay_send,
     half_send, half_recv, quarter_send, quarter_recv, share_send, share_recv) = rest[5 * count:]
    depth, width = dose.shape
    chunks = width // LANES
    quarter = width // 4
    samples = 4 * depth
    v = lax.axis_index("var")
    s = lax.axis_index("samp")
    core = lax.rem(s, 2)
    side = s // 2
    y = lax.rem(v, RING)
    edge = lax.rem(v, chain // 2) < RING
    leaves = jnp.logical_and(edge, y != RING - 1)
    first_in_ring = y == 0
    last_in_ring = y == RING - 1

    def at(step, member=None):
        return (lax.rem(v + step + chain, chain), s if member is None else member)

    mate = (v, s + 1 - 2 * core)
    opposite = (v, lax.rem(s + 2, 4))

    def cols(j):
        return pl.ds(j * LANES, LANES)

    loads = []
    for j in range(chunks):
        loads.append((
            pltpu.make_async_copy(dose_hbm.at[:, cols(j)], dose.at[:, cols(j)], load_sem.at[0, j]),
            pltpu.make_async_copy(seen_hbm.at[:, cols(j)], seen.at[:, cols(j)], load_sem.at[1, j])))
        for copy in loads[-1]:
            copy.start()

    barrier = pltpu.get_barrier_semaphore()
    friends = [(v, lax.rem(s + k, 4)) for k in (1, 2, 3)]
    for step in (1, 3):
        friends += [at(step, q) for q in range(4)] + [at(-step, q) for q in range(4)]
    friends += [at(4), at(-4)]
    across = chain // 2
    if across > 4:
        friends += [at(step) for step in (across, across + 3, -across - 3, across - 4, 4 - across)]
    for friend in friends:
        pl.semaphore_signal(barrier, inc=1, device_id=friend, device_id_type=MESH)

    row_own[...] = jnp.zeros_like(row_own)
    row_near[...] = jnp.zeros_like(row_near)
    col_near[...] = jnp.zeros_like(col_near)
    col_far[...] = jnp.zeros_like(col_far)

    block = min(256, depth)

    def sum_chunk(j):
        def body(r, acc):
            rows = pl.ds(pl.multiple_of(r * block, block), block)
            present = seen[rows, cols(j)].astype(F32)
            values = dose[rows, cols(j)].astype(F32)
            weighted = present * values
            terms = (present, weighted, weighted * values)
            return tuple(a + jnp.sum(t.reshape(block // 8, 8, LANES), 0) for a, t in zip(acc, terms))

        zero = jnp.zeros((8, LANES), F32)
        sums = lax.fori_loop(0, depth // block, body, (zero, zero, zero))
        for i, total in enumerate(sums):
            stat[j, i:i + 1, :] = jnp.sum(total, 0, keepdims=True)

    def stat_copy(j, k):
        return pltpu.make_async_remote_copy(
            src_ref=stat.at[j], dst_ref=stat_in.at[k - 1, j], send_sem=stat_send.at[k - 1, j],
            recv_sem=stat_recv.at[k - 1, j], device_id=(v, lax.rem(s + k, 4)), device_id_type=MESH)

    def piece(ref, j, p):
        rows = depth // PIECES
        return ref.at[pl.ds(p * rows, rows), cols(j)]

    def halves(j):
        return (0, 1) if j == chunks - 1 else (0,)

    def span(ref, j, h):
        rows = depth // len(halves(j))
        return ref.at[pl.ds(h * rows, rows), cols(j)]

    def slot(j, p):
        return j + p // (PIECES // len(halves(j)))

    def near_copy(j, h):
        return pltpu.make_async_remote_copy(
            src_ref=span(own, j, h), dst_ref=span(near, j, h), send_sem=near_send.at[j + h],
            recv_sem=near_recv.at[j + h], device_id=at(-1), device_id_type=MESH)

    def hop_copy(j, p):
        return pltpu.make_async_remote_copy(
            src_ref=piece(own, j, p), dst_ref=piece(relay, j, p), send_sem=hop_send.at[j, p],
            recv_sem=hop_recv.at[j, p], device_id=at(jnp.where(edge, across + 3, 3) if p < NEAR_SIDE else 3), device_id_type=MESH)

    def relay_copy(j, p, target, sem, step):
        return pltpu.make_async_remote_copy(
            src_ref=piece(relay, j, p), dst_ref=piece(target, j, p), send_sem=relay_send.at[j, p],
            recv_sem=sem.at[slot(j, p)], device_id=at(step), device_id_type=MESH)

    def near_relay(j, p):
        return relay_copy(j, p, near, near_recv, jnp.where(edge, across - 4, -4) if p < NEAR_SIDE else -4)

    def far_relay(j, p):
        return relay_copy(j, p, far, far_recv, across - 3)

    def far_copy(j, h):
        return pltpu.make_async_remote_copy(
            src_ref=span(own, j, h), dst_ref=span(far, j, h), send_sem=far_send.at[j + h],
            recv_sem=far_recv.at[j + h], device_id=at(-3), device_id_type=MESH)

    def direct_copy(j, p):
        return pltpu.make_async_remote_copy(
            src_ref=piece(own, j, p), dst_ref=piece(far, j, p), send_sem=edge_send.at[j, p],
            recv_sem=far_recv.at[slot(j, p)], device_id=at(-3), device_id_type=MESH)

    def cross_copy(j, p):
        return pltpu.make_async_remote_copy(
            src_ref=piece(own, j, p), dst_ref=piece(relay, j, p), send_sem=edge_send.at[j, p],
            recv_sem=hop_recv.at[j, p], device_id=at(across), device_id_type=MESH)

    def by_side(act_side, act_straight):
        for here, count_side in ((first_in_ring, FAR_SIDE[0]), (jnp.logical_not(first_in_ring), FAR_SIDE[1])):
            @pl.when(jnp.logical_and(leaves, here))
            def _(count_side=count_side):
                for p in range(PIECES):
                    (act_side if p < count_side else act_straight)(p)

    def each_direct(j, act):
        by_side(lambda p: None, lambda p: act(direct_copy(j, p)))

    def each_send(j, act):
        @pl.when(jnp.logical_not(leaves))
        def _():
            for h in halves(j):
                act(far_copy(j, h))

        by_side(lambda p: act(cross_copy(j, p)), lambda p: None)

        @pl.when(first_in_ring)
        def _():
            for p in range(PIECES):
                act(hop_copy(j, p))

        @pl.when(jnp.logical_not(first_in_ring))
        def _():
            for h in halves(j):
                act(near_copy(j, h))

    def standardize(j):
        for k in (1, 2, 3):
            stat_copy(j, k).wait_recv()
        sums = stat[j] + stat_in[0, j] + stat_in[1, j] + stat_in[2, j]
        seen_count = jnp.maximum(sums[0:1], 1.0)
        mean = sums[1:2] / seen_count
        spread = sums[2:3] / seen_count - mean * mean
        scale = lax.rsqrt(spread + 1e-05)

        def body(r, carry):
            rows = pl.ds(pl.multiple_of(r * block, block), block)
            present = seen[rows, cols(j)].astype(F32)
            values = dose[rows, cols(j)].astype(F32)
            own[rows, cols(j)] = ((values - mean) * scale * present).astype(BF16)
            return carry

        lax.fori_loop(0, depth // block, body, 0)

        each_send(j, lambda copy: copy.start())
        if j < 2:
            each_direct(j, lambda copy: copy.start())

    hops = [(j, p) for j in range(chunks) for p in range(PIECES)]
    passed = []

    def pass_on(until):
        ready = [hop for hop in hops if hop < until and hop not in passed]
        passed.extend(ready)

        @pl.when(last_in_ring)
        def _():
            for j, p in ready:
                hop_copy(j, p).wait_recv()
                near_relay(j, p).start()

        for j, q in ready:
            def hand_on(p):
                if p == q:
                    hop_copy(j, p).wait_recv()
                    far_relay(j, p).start()

            by_side(hand_on, lambda p: None)

        for j, p in ready:
            if p == 1 and j + 2 < chunks:
                each_direct(j + 2, lambda copy: copy.start())

    for j in range(chunks + 2):
        if j < chunks:
            for copy in loads[j]:
                copy.wait()
            stat[j] = jnp.zeros((8, LANES), F32)
            sum_chunk(j)
            if j == 0:
                pl.semaphore_wait(barrier, len(friends))
            for k in (1, 2, 3):
                stat_copy(j, k).start()
        if j >= 2:
            standardize(j - 2)
        if j >= chunks:
            pass_on((0, j - chunks + 1))

    keep_near = jnp.where(v + 1 < chain, 1.0, 0.0).astype(F32)
    keep_far = jnp.where(v + 3 < chain, 1.0, 0.0).astype(F32)
    keep_cross = jnp.where(lax.rem(v + 1, chain) + 2 < chain, 1.0, 0.0).astype(F32)

    def dot(a, b):
        return lax.dot_general(a, b, (((0,), (0,)), ((), ())), preferred_element_type=F32)

    def half_copy(u):
        return pltpu.make_async_remote_copy(
            src_ref=half_out[u], dst_ref=half_in[u], send_sem=half_send.at[u], recv_sem=half_recv.at[u],
            device_id=mate, device_id_type=MESH)

    def quarter_copy(u):
        return pltpu.make_async_remote_copy(
            src_ref=quarter_out[u], dst_ref=quarter_in[u], send_sem=quarter_send.at[u],
            recv_sem=quarter_recv.at[u], device_id=opposite, device_id_type=MESH)

    def rows_of(u, index):
        size = units[u][2] // 4
        return pl.ds(pl.multiple_of(index * size, size), size)

    def multiply(u, h, last):
        kind, j, _, _ = units[u]
        rows = slice(None) if last and h == 0 else slice(h * depth // 2, (h + 1) * depth // 2)
        if kind == "own":
            product = dot(own[rows, :], own[rows, 2 * j * LANES:2 * (j + 1) * LANES])
        elif kind == "both":
            product = dot(own[rows, :], jnp.concatenate([near[rows, cols(j)], far[rows, cols(j)]], 1))
        elif kind == "down":
            product = dot(near[rows, :LANES * (j + 1)], far[rows, cols(j)])
        else:
            product = dot(near[rows, cols(j)], far[rows, :LANES * j])
        part[u][...] = part[u][...] + product if h else product
        if last:
            for p in range(2):
                half_out[u][p] = part[u][rows_of(u, 2 * p + 1 - core), :].astype(BF16)
            half_copy(u).start()

    def fold_mate(u):
        half_copy(u).wait_recv()
        away = rows_of(u, 2 * (1 - side) + core)
        quarter_out[u][...] = (part[u][away, :] + half_in[u][1 - side].astype(F32)).astype(BF16)
        quarter_copy(u).start()
        home = rows_of(u, s)
        part[u][home, :] = part[u][home, :] + half_in[u][side].astype(F32)

    def by_lane(x):
        total = x[:, :LANES]
        for i in range(1, x.shape[1] // LANES):
            total = total + x[:, i * LANES:(i + 1) * LANES]
        return total

    def by_sublane(x):
        return jnp.sum(x.reshape(x.shape[0] // 8, 8, x.shape[1]), 0)

    def fold_opposite(u):
        quarter_copy(u).wait_recv()
        kind, j, rows, columns = units[u]
        total = part[u][rows_of(u, s), :] + quarter_in[u][...].astype(F32)
        square = total * total
        if kind == "own":
            row_own[:quarter, :] += by_lane(square)
        elif kind == "both":
            to_near = square[:, :LANES] * keep_near
            to_far = square[:, LANES:] * keep_far
            row_own[:quarter, :] += to_near + to_far
            col_near[:, cols(j)] += by_sublane(to_near)
            col_far[:, cols(j)] += by_sublane(to_far)
        else:
            square = square * keep_cross
            size = rows // 4
            start = s * size if kind == "down" else LANES * j + s * size
            where = pl.ds(pl.multiple_of(start, size), size)
            row_near[where, :] += by_lane(square)
            if kind == "down":
                col_far[:, cols(j)] += by_sublane(square)
            else:
                col_far[:, :columns] += by_sublane(square)

    groups = [[u for u in range(count) if units[u][0] == "own"]]
    for j in range(chunks):
        groups.append([u for u in range(count) if units[u][0] != "own" and units[u][1] == j])
    to_mate, to_opposite = [], []

    def drain(group):
        while to_opposite and to_opposite[0][0] <= group:
            fold_opposite(to_opposite.pop(0)[1])

    for g, group in enumerate(groups):
        parts = halves(g - 1)
        if g == chunks:
            while to_mate:
                done = to_mate.pop(0)
                fold_mate(done[1])
                to_opposite.append(done)
        for h in parts:
            if g:
                if h == 0:
                    pass_on((g, PIECES - 1))
                far_copy(g - 1, h).wait_recv()
                near_copy(g - 1, h).wait_recv()
            last = h == parts[-1]
            for i, u in enumerate(group):
                multiply(u, h, last)
                if not last:
                    continue
                if to_mate:
                    done = to_mate.pop(0)
                    fold_mate(done[1])
                    to_opposite.append(done)
                to_mate.append((g, u))
                pass_on((g, i + 2))
                drain(g - 4)
        pass_on((g, PIECES))
    for done in to_mate:
        fold_mate(done[1])
        to_opposite.append(done)
    drain(chunks)

    near_sum = jnp.sum(row_near[...].T, 0, keepdims=True) + jnp.sum(col_near[...], 0, keepdims=True)
    far_sum = jnp.sum(col_far[...], 0, keepdims=True)

    def share_copy(i, q):
        return pltpu.make_async_remote_copy(
            src_ref=share.at[i, q], dst_ref=share_in.at[i, s], send_sem=share_send.at[i, q],
            recv_sem=share_recv.at[i, s], device_id=at((1, 3)[i], q), device_id_type=MESH)

    def share_arrival(i, q):
        return pltpu.make_async_remote_copy(
            src_ref=share.at[i, q], dst_ref=share_in.at[i, q], send_sem=share_send.at[i, q],
            recv_sem=share_recv.at[i, q], device_id=at((1, 3)[i], q), device_id_type=MESH)

    for i, total in enumerate((near_sum, far_sum)):
        wide = jnp.broadcast_to(total, (8, width))
        for q in range(4):
            turned = wide if q == 0 else pltpu.roll(wide, width - q * quarter, 1)
            share[i, q] = turned[0:1, :2 * LANES]
            share_copy(i, q).start()
    row_total = jnp.sum(row_own[...].T, 0, keepdims=True)
    for i in range(2):
        for q in range(4):
            share_arrival(i, q).wait_recv()
            row_total = row_total + share_in[i, q]
    pairs = (1 + jnp.minimum(v, BAND) + jnp.minimum(chain - 1 - v, BAND)).astype(F32)
    squares = row_total * (1.0 / (samples * samples))
    result = squares / width + (squares / width - pairs) / (samples - 2)
    out_ref[...] = result[:, :quarter]

    for j in range(chunks):
        for k in (1, 2, 3):
            stat_copy(j, k).wait_send()
        each_send(j, lambda copy: copy.wait_send())
        each_direct(j, lambda copy: copy.wait_send())

    @pl.when(last_in_ring)
    def _():
        for j, p in hops:
            near_relay(j, p).wait_send()

    for j in range(chunks):
        by_side(lambda p: far_relay(j, p).wait_send(), lambda p: None)

    for u in range(count):
        half_copy(u).wait_send()
        quarter_copy(u).wait_send()
    for i in range(2):
        for q in range(4):
            share_copy(i, q).wait_send()


def local(chain, dosages, observed):
    depth, width = dosages.shape
    chunks = width // LANES
    units = plan(chunks)
    count = len(units)
    dma = pltpu.SemaphoreType.DMA
    scratch = [
        pltpu.VMEM((depth, width), BF16),
        pltpu.VMEM((depth, width), jnp.int32),
        pltpu.VMEM((depth, width), BF16),
        pltpu.VMEM((depth, width), BF16),
        pltpu.VMEM((depth, width), BF16),
        pltpu.VMEM((depth, width), BF16),
        pltpu.VMEM((chunks, 8, LANES), F32),
        pltpu.VMEM((3, chunks, 8, LANES), F32),
        pltpu.VMEM((2 * LANES, LANES), F32),
        pltpu.VMEM((width, LANES), F32),
        pltpu.VMEM((8, width), F32),
        pltpu.VMEM((8, width), F32),
        pltpu.VMEM((2, 4, 1, 2 * LANES), F32),
        pltpu.VMEM((2, 4, 1, 2 * LANES), F32),
    ]
    scratch += [pltpu.VMEM((rows, columns), F32) for _, _, rows, columns in units]
    for _ in range(2):
        scratch += [pltpu.VMEM((2, rows // 4, columns), BF16) for _, _, rows, columns in units]
    for _ in range(2):
        scratch += [pltpu.VMEM((rows // 4, columns), BF16) for _, _, rows, columns in units]
    scratch += [
        dma((2, chunks)), dma((3, chunks)), dma((3, chunks)),
        dma((chunks + 1,)), dma((chunks + 1,)), dma((chunks + 1,)), dma((chunks + 1,)),
        dma((chunks, PIECES)), dma((chunks, PIECES)), dma((chunks, PIECES)), dma((chunks, PIECES)),
        dma((count,)), dma((count,)), dma((count,)), dma((count,)),
        dma((2, 4)), dma((2, 4)),
    ]
    out = pl.pallas_call(
        functools.partial(kernel, chain, units),
        out_shape=jax.ShapeDtypeStruct((1, width // 4), F32),
        in_specs=[pl.BlockSpec(memory_space=pl.ANY)] * 2,
        out_specs=pl.BlockSpec(memory_space=pltpu.VMEM),
        scratch_shapes=scratch,
        compiler_params=pltpu.CompilerParams(
            collective_id=0, has_side_effects=True, vmem_limit_bytes=56 * 2**20),
    )(dosages, observed)
    return out.reshape(width // 4)


def solution(mesh):
    placed = (P("samp", "var"), P("samp", "var"))
    return jax.shard_map(
        functools.partial(local, mesh.shape["var"]), mesh=mesh, in_specs=placed,
        out_specs=P(("var", "samp")), check_vma=False)
```
